1024 devices in a mesh: blk: 64 (over x, y, core), mp: 8 (over z_lo), tower: 2 (over z_hi).
Axes of the slice: x: 4, y: 8, z: 16 (z_hi: 2, z_lo: 8; z = z_hi * 8 + z_lo), core: 2. Of those that a mesh axis runs over, the one named last changes fastest.
Arguments:
- image_features: bfloat16 [16384, 1536], P('blk'), may hold values from -12 to 12
- text_features: bfloat16 [16384, 1024], P('blk'), may hold values from -12 to 12
- image_head: bfloat16 [1536, 1024], P(None, 'mp')
- text_head: bfloat16 [1024, 1024], P(None, 'mp')
- positive: int32 [16384], replicated, may hold values from 0 to 16383, as said below
- log_scale: float32 [1], replicated, may hold values from 1.4 to 2.3
- bias: float32 [1], replicated, may hold values from -4 to -2
Outputs:
- embed_grads: float32 [2, 16384, 1024], P('tower', 'blk', 'mp')
The draws below stay inside these ranges and needn't reach their ends.
Inputs may be any that keep to these rules, and one draw needn't show every extreme that they name: `positive`: each text index appears exactly once.
All inputs are finite; a program needn't handle non-finite values.
Results may differ from the reference program's by a relative error of at most 0.0015.
Values may be sent and summed in bfloat16 or wider, within the bound.
No kernel may reach another device: no remote copies, remote signals or barrier semaphores. Data moves between devices by JAX's collectives and lax.ppermute only.
A program may use at most 32 MiB of HBM per device.

```python
import math
import jax
import jax.numpy as jnp
from jax import lax

IMAGE_WIDTH = 1536
TEXT_WIDTH = 1024
EMBED = 1024
ROWS = 256
BATCH = 16384
N_BLK = 64


def column_factors(key):
    key = jax.random.fold_in(key, 5)
    return jnp.exp(jax.random.uniform(key, (EMBED,), jnp.float32, 0.0, math.log(10.0)))


def pair_order(key):
    key = jax.random.fold_in(key, 7)
    return jax.random.permutation(key, BATCH).astype(jnp.int32)


def shared_latent(key, cluster_share):
    groups = max(BATCH // 64, 2)
    member = jax.random.randint(jax.random.fold_in(key, 9), (BATCH,), 0, groups)
    centers = jax.random.normal(jax.random.fold_in(key, 13), (groups, EMBED), jnp.float32)
    single = jax.random.normal(jax.random.fold_in(key, 17), (BATCH, EMBED), jnp.float32)
    return math.sqrt(cluster_share) * centers[member] + math.sqrt(1.0 - cluster_share) * single


def make_head(random_part, rows_count, factors):
    diagonal = (jnp.arange(rows_count)[:, None] == jnp.arange(EMBED)[None, :]).astype(jnp.float32)
    mixed = diagonal + 0.5 * random_part / math.sqrt(rows_count)
    return mixed * factors[None, :] / math.sqrt(20.0 * EMBED)


def mix_features(signal, jitter, row_factor, feature_count):
    column_mask = jnp.arange(feature_count)[None, :] < EMBED
    jitter_weight = jnp.where(column_mask, 0.5, 1.0)
    return jnp.clip((signal + jitter * jitter_weight) * row_factor, -12.0, 12.0)


def draw_positive(key, part):
    return pair_order(key)


def draw_image_features(key, part):
    pairing = pair_order(key)
    latent = shared_latent(key, 0.45)
    key = jax.random.fold_in(key, 31)
    noise_key, scale_key = jax.random.split(key)
    jitter = jax.random.normal(noise_key, (BATCH, IMAGE_WIDTH), jnp.float32)
    spread = math.log(2.0)
    row_factor = jnp.exp(jax.random.uniform(scale_key, (BATCH, 1), jnp.float32, -spread, spread))
    signal = jnp.pad(latent[pairing], ((0, 0), (0, IMAGE_WIDTH - EMBED)))
    return mix_features(signal, jitter, row_factor, IMAGE_WIDTH).astype(jnp.bfloat16)


def draw_text_features(key, part):
    latent = shared_latent(key, 0.45)
    key = jax.random.fold_in(key, 37)
    noise_key, scale_key = jax.random.split(key)
    jitter = jax.random.normal(noise_key, (BATCH, TEXT_WIDTH), jnp.float32)
    spread = math.log(2.0)
    row_factor = jnp.exp(jax.random.uniform(scale_key, (BATCH, 1), jnp.float32, -spread, spread))
    signal = jnp.pad(latent, ((0, 0), (0, TEXT_WIDTH - EMBED)))
    return mix_features(signal, jitter, row_factor, TEXT_WIDTH).astype(jnp.bfloat16)


def draw_image_head(key, part):
    factors = column_factors(key)
    key = jax.random.fold_in(key, 11)
    random_part = jnp.clip(jax.random.normal(key, (IMAGE_WIDTH, EMBED), jnp.float32), -6.0, 6.0)
    return make_head(random_part, IMAGE_WIDTH, factors).astype(jnp.bfloat16)


def draw_text_head(key, part):
    factors = column_factors(key)
    key = jax.random.fold_in(key, 23)
    random_part = jnp.clip(jax.random.normal(key, (TEXT_WIDTH, EMBED), jnp.float32), -6.0, 6.0)
    return make_head(random_part, TEXT_WIDTH, factors).astype(jnp.bfloat16)


def setup_inputs(seed: int = 0) -> dict:
    arg_keys = jax.random.split(jax.random.key(seed), 8)
    return {
        "image_features": draw_image_features(jax.random.fold_in(arg_keys[7], 71), 0),
        "text_features": draw_text_features(jax.random.fold_in(arg_keys[7], 71), 0),
        "image_head": draw_image_head(jax.random.fold_in(arg_keys[7], 71), 0),
        "text_head": draw_text_head(jax.random.fold_in(arg_keys[7], 71), 0),
        "positive": draw_positive(jax.random.fold_in(arg_keys[7], 71), 0),
        "log_scale": jnp.clip(jax.random.uniform(arg_keys[5], (1,), jnp.float32, 1.4, 2.3), 1.4, 2.3),
        "bias": jnp.clip(jax.random.uniform(arg_keys[6], (1,), jnp.float32, -4.0, -2.0), -4.0, -2.0),
    }


def normalize(embed):
    norm = jnp.sqrt(lax.optimization_barrier(jnp.sum(embed * embed, axis=1, keepdims=True)) + 1e-06)
    return (embed / norm, norm)

def unit_grads(own_b, own_key, other_b, other_key, scale, offset):
    blocks = own_b.reshape(N_BLK, ROWS, EMBED)
    keys = own_key.reshape(N_BLK, ROWS)

    def one_block(pair):
        zb_block, key_block = pair
        logits = scale * jnp.dot(zb_block, other_b.T, preferred_element_type=jnp.float32) + offset
        sign = jnp.where(key_block[:, None] == other_key[None, :], 1.0, -1.0)
        weight = (-sign * jax.nn.sigmoid(-sign * logits) * scale).astype(jnp.bfloat16)
        return jnp.dot(weight, other_b, preferred_element_type=jnp.float32)
    return lax.map(one_block, (blocks, keys)).reshape(BATCH, EMBED)

def reference(image_features, text_features, image_head, text_head, positive, log_scale, bias):
    image_embed = jnp.dot(image_features, image_head, preferred_element_type=jnp.float32)
    text_embed = jnp.dot(text_features, text_head, preferred_element_type=jnp.float32)
    image_unit, image_norm = normalize(image_embed)
    text_unit, text_norm = normalize(text_embed)
    image_b = image_unit.astype(jnp.bfloat16)
    text_b = text_unit.astype(jnp.bfloat16)
    scale = jnp.exp(log_scale[0])
    offset = bias[0]
    text_index = jnp.arange(BATCH, dtype=jnp.int32)
    image_grad = unit_grads(image_b, positive, text_b, text_index, scale, offset)
    text_grad = unit_grads(text_b, text_index, image_b, positive, scale, offset)
    image_out = (image_grad - image_unit * lax.optimization_barrier(jnp.sum(image_unit * image_grad, axis=1, keepdims=True))) / image_norm
    text_out = (text_grad - text_unit * lax.optimization_barrier(jnp.sum(text_unit * text_grad, axis=1, keepdims=True))) / text_norm
    return jnp.stack([image_out, text_out])
```

```python
import jax
import jax.numpy as jnp
from jax import lax
from jax.sharding import Mesh, PartitionSpec as P

BLK = ("x", "ya", "yb", "c")
AXES = BLK + ("zl", "zh")
COLUMN = ("zh", "zl")
IMAGE_GROUP = ("x", "yb")
F32 = jnp.float32


def spread(value, axis):
    count = lax.axis_size(axis)
    copies = jnp.broadcast_to(value[None], (count,) + value.shape)
    return lax.all_to_all(copies, axis, 0, 0, tiled=True)


def summed(parts, axis):
    count = lax.axis_size(axis)
    parts = parts.reshape((count, -1) + parts.shape[1:])
    return jnp.sum(lax.all_to_all(parts, axis, 0, 0, tiled=True).astype(F32), axis=0)


def swapped(value):
    return lax.ppermute(value, "c", [(0, 1), (1, 0)])


def normalize(embed):
    norm = jnp.sqrt(jnp.sum(embed * embed, axis=1, keepdims=True) + 1e-06)
    return embed / norm, norm


def projected(grad, unit, norm):
    return (grad - unit * jnp.sum(unit * grad, axis=1, keepdims=True)) / norm


def shards(image_features, text_features, image_head, text_head, positive, log_scale, bias):
    rows = image_features.shape[0]
    planes = lax.axis_size(COLUMN)
    lanes = lax.axis_size("zl")
    quarter = rows // 4
    half = quarter // 2
    x, ya, yb, c = (lax.axis_index(name) for name in BLK)
    zh = lax.axis_index("zh")
    plane = zh * lanes + lax.axis_index("zl")
    image_part, text_part = plane // 4, plane % 4
    scale = jnp.exp(log_scale[0])
    offset = bias[0]

    def head_part(features, head):
        own = features.reshape(4, 2, half, -1)
        own = lax.dynamic_index_in_dim(own, zh, 1, keepdims=False).reshape(4 * half, -1)
        return jnp.dot(own, head, preferred_element_type=F32).reshape(4, half, -1)

    image_cols = head_part(image_features, image_head)
    text_cols = head_part(text_features, text_head)
    width = image_cols.shape[-1]
    pieces = jnp.concatenate(
        [
            jnp.broadcast_to(image_cols[:, None], (4, 4, half, width)),
            jnp.broadcast_to(text_cols[None], (4, 4, half, width)),
        ],
        axis=2,
    ).reshape(planes, 2 * half, width)
    pieces = lax.all_to_all(pieces, COLUMN, 0, 0, tiled=True)
    pieces = pieces.reshape(2, lanes, 2, half, width)
    whole = pieces.transpose(2, 0, 3, 1, 4).reshape(2, quarter, lanes * width)
    image_unit, image_norm = normalize(whole[0])
    text_unit, text_norm = normalize(whole[1])

    text_own = spread(text_unit.astype(jnp.bfloat16), "ya").reshape(4 * quarter, -1)
    text_far = swapped(text_own)
    image_b = spread(image_unit.astype(jnp.bfloat16), IMAGE_GROUP).reshape(8 * quarter, -1)

    keys = positive.reshape(4, 4, 2, 2, 4, quarter)
    keys = lax.dynamic_slice(keys, (0, ya, 0, c, image_part, 0), (4, 1, 2, 1, 1, quarter))
    keys = keys.reshape(8 * quarter)

    def text_index(core):
        block = ((x * 4 + jnp.arange(4, dtype=jnp.int32)) * 2 + yb) * 2 + core
        start = block * rows + text_part * quarter
        return (start[:, None] + jnp.arange(quarter, dtype=jnp.int32)[None]).reshape(-1)

    def weights(text_b, index):
        logits = scale * jnp.einsum("re,ce->rc", image_b, text_b, preferred_element_type=F32)
        logits = logits + offset
        sign = jnp.where(keys[:, None] == index[None, :], 1.0, -1.0)
        return (-sign * jax.nn.sigmoid(-sign * logits) * scale).astype(jnp.bfloat16)

    def to_texts(weight):
        return jnp.einsum("rc,re->ce", weight, image_b, preferred_element_type=F32)

    def to_images(weight, text_b):
        return jnp.dot(weight, text_b, preferred_element_type=F32)

    weight_far = weights(text_far, text_index(1 - c))
    far_grad = swapped(to_texts(weight_far))
    weight_own = weights(text_own, text_index(c))
    image_grad = to_images(weight_far, text_far) + to_images(weight_own, text_own)
    text_grad = to_texts(weight_own) + far_grad

    image_grad = summed(image_grad.astype(jnp.bfloat16), IMAGE_GROUP)
    text_grad = summed(text_grad.astype(jnp.bfloat16), "ya")
    both = jnp.stack(
        [projected(image_grad, image_unit, image_norm), projected(text_grad, text_unit, text_norm)]
    )
    both = both.reshape(2, quarter, lanes, width).transpose(0, 2, 1, 3)
    both = lax.all_to_all(both.reshape(planes, quarter, width), COLUMN, 0, 0, tiled=True)
    both = both.reshape(4, 4, quarter, width)
    result = jnp.where(zh == 0, jnp.sum(both, axis=1), jnp.sum(both, axis=0))
    return result.reshape(1, rows, width)


def solution(mesh):
    fine = Mesh(mesh.devices.reshape(4, 4, 2, 2, 8, 2), AXES)
    placed = (P(BLK, None), P(BLK, None), P(None, "zl"), P(None, "zl"), P(), P(), P())
    return jax.shard_map(
        shards, mesh=fine, in_specs=placed, out_specs=P("zh", BLK, "zl"), check_vma=False
    )
```

```python
import jax
import jax.numpy as jnp
from jax import lax
from jax.sharding import Mesh, PartitionSpec as P

BLK = ("x", "ya", "yb", "c")
AXES = BLK + ("zl", "zh")
COLUMN = ("zh", "zl")
IMAGE_GROUP = ("x", "yb")
F32 = jnp.float32


def spread(value, axis):
    count = lax.axis_size(axis)
    copies = jnp.broadcast_to(value[None], (count,) + value.shape)
    return lax.all_to_all(copies, axis, 0, 0, tiled=True)


def summed(parts, axis):
    count = lax.axis_size(axis)
    parts = parts.reshape((count, -1) + parts.shape[1:])
    return jnp.sum(lax.all_to_all(parts, axis, 0, 0, tiled=True).astype(F32), axis=0)


def swapped(value):
    return lax.ppermute(value, "c", [(0, 1), (1, 0)])


def shifted(value, axis, steps):
    count = lax.axis_size(axis)
    return lax.ppermute(value, axis, [(k, (k + steps) % count) for k in range(count)])


def floor_power(value):
    return jnp.floor(jnp.log2(value))


def normalize(embed):
    norm = jnp.sqrt(jnp.sum(embed * embed, axis=1, keepdims=True) + 1e-06)
    return embed / norm, norm


def projected(grad, unit):
    return grad - unit * jnp.sum(unit * grad, axis=1, keepdims=True)


def shards(image_features, text_features, image_head, text_head, positive, log_scale, bias):
    rows = image_features.shape[0]
    planes = lax.axis_size(COLUMN)
    lanes = lax.axis_size("zl")
    quarter = rows // 4
    half = quarter // 2
    x, ya, yb, c = (lax.axis_index(name) for name in BLK)
    zh = lax.axis_index("zh")
    plane = zh * lanes + lax.axis_index("zl")
    image_part, text_part = plane // 4, plane % 4
    scale = jnp.exp(log_scale[0])
    offset = bias[0]

    def head_part(features, head):
        own = features.reshape(4, 2, half, -1)
        own = lax.dynamic_index_in_dim(own, zh, 1, keepdims=False).reshape(4 * half, -1)
        return jnp.dot(own, head, preferred_element_type=F32).reshape(4, half, -1)

    image_cols = head_part(image_features, image_head)
    text_cols = head_part(text_features, text_head)
    width = image_cols.shape[-1]
    pieces = jnp.concatenate(
        [
            jnp.broadcast_to(image_cols[:, None], (4, 4, half, width)),
            jnp.broadcast_to(text_cols[None], (4, 4, half, width)),
        ],
        axis=2,
    ).reshape(planes, 2 * half, width)
    pieces = lax.all_to_all(pieces, COLUMN, 0, 0, tiled=True)
    pieces = pieces.reshape(2, lanes, 2, half, width)
    whole = pieces.transpose(2, 0, 3, 1, 4).reshape(2, quarter, lanes * width)
    image_unit, image_norm = normalize(whole[0])
    text_unit, text_norm = normalize(whole[1])

    text_b = text_unit.astype(jnp.bfloat16)
    text_own = jnp.concatenate([text_b] + [shifted(text_b, "ya", k) for k in range(1, 4)])
    text_far = swapped(text_own)
    image_b = spread(image_unit.astype(jnp.bfloat16), IMAGE_GROUP).reshape(8 * quarter, -1)

    keys = positive.reshape(4, 4, 2, 2, 4, quarter)
    keys = lax.dynamic_slice(keys, (0, ya, 0, c, image_part, 0), (4, 1, 2, 1, 1, quarter))
    keys = keys.reshape(8 * quarter)

    def text_index(core):
        block = ((x * 4 + (ya - jnp.arange(4, dtype=jnp.int32)) % 4) * 2 + yb) * 2 + core
        start = block * rows + text_part * quarter
        return (start[:, None] + jnp.arange(quarter, dtype=jnp.int32)[None]).reshape(-1)

    def weights(text_b, index):
        logits = scale * jnp.einsum("re,ce->rc", image_b, text_b, preferred_element_type=F32)
        logits = logits + offset
        sign = jnp.where(keys[:, None] == index[None, :], 1.0, -1.0)
        return (-sign * jax.nn.sigmoid(-sign * logits) * scale).astype(jnp.bfloat16)

    def to_texts(weight):
        return jnp.einsum("rc,re->ce", weight, image_b, preferred_element_type=F32)

    def to_images(weight, text_b):
        return jnp.dot(weight, text_b, preferred_element_type=F32)

    weight_far = weights(text_far, text_index(1 - c))
    far_grad = swapped(to_texts(weight_far))
    weight_own = weights(text_own, text_index(c))
    image_grad = to_images(weight_far, text_far) + to_images(weight_own, text_own)
    text_grad = to_texts(weight_own) + far_grad

    text_parts = text_grad.astype(jnp.float16).reshape(4, quarter, -1)
    text_grad = text_parts[0].astype(F32)
    for k in range(1, 4):
        text_grad = text_grad + shifted(text_parts[k], "ya", -k).astype(F32)
    image_grad = summed(image_grad.astype(jnp.float16), IMAGE_GROUP)

    both = jnp.stack([projected(image_grad, image_unit), projected(text_grad, text_unit)])
    norms = jnp.stack([image_norm, text_norm])
    powers = floor_power(norms)
    both = (both * (jnp.exp2(powers) / norms)).astype(jnp.float16)
    both = both.reshape(2, quarter, lanes, width).transpose(0, 2, 1, 3)
    powers = jnp.pad(powers.reshape(2, 1, quarter), ((0, 0), (0, 15), (0, width - quarter)))
    powers = jnp.broadcast_to(powers[:, None], (2, lanes, 16, width)).astype(jnp.float16)
    both = jnp.concatenate([both, powers], axis=2).reshape(planes, quarter + 16, width)
    both = lax.all_to_all(both, COLUMN, 0, 0, tiled=True)
    powers = both[:, quarter, :quarter].astype(F32).reshape(4, 4, quarter)
    powers = jnp.where(zh == 0, powers[:, 0], powers[0])
    both = both[:, :quarter].astype(F32).reshape(4, 4, quarter, width)
    result = jnp.where(zh == 0, jnp.sum(both, axis=1), jnp.sum(both, axis=0))
    result = result / jnp.exp2(powers)[:, :, None]
    return result.reshape(1, rows, width)


def solution(mesh):
    fine = Mesh(mesh.devices.reshape(4, 4, 2, 2, 8, 2), AXES)
    placed = (P(BLK, None), P(BLK, None), P(None, "zl"), P(None, "zl"), P(), P(), P())
    return jax.shard_map(
        shards, mesh=fine, in_specs=placed, out_specs=P("zh", BLK, "zl"), check_vma=False
    )
```

```python
import jax
import jax.numpy as jnp
from jax import lax
from jax.sharding import Mesh, PartitionSpec as P

BLK = ("x", "y", "c")
AXES = BLK + ("zl", "zh")
COLUMN = ("zh", "zl")
F32 = jnp.float32
HALF = jnp.float16


def spread(value, axis):
    count = lax.axis_size(axis)
    copies = jnp.broadcast_to(value[None], (count,) + value.shape)
    return lax.all_to_all(copies, axis, 0, 0, tiled=True)


def summed(parts, axis):
    count = lax.axis_size(axis)
    parts = parts.reshape((count, -1) + parts.shape[1:])
    return jnp.sum(lax.all_to_all(parts, axis, 0, 0, tiled=True).astype(F32), axis=0)


def swapped(value):
    return lax.ppermute(value, "c", [(0, 1), (1, 0)])


def shifted(value, axis, steps):
    count = lax.axis_size(axis)
    return lax.ppermute(value, axis, [(k, (k + steps) % count) for k in range(count)])


def exponent(value):
    return jnp.clip(jnp.floor(jnp.log2(jnp.maximum(value, 1e-30))), -100.0, 126.0)


def with_exponents(rows, powers):
    count, width = rows.shape[-2:]
    lead = [(0, 0)] * (powers.ndim - 1)
    powers = jnp.pad(powers[..., None, :], lead + [(0, 7), (0, width - count)])
    powers = jnp.broadcast_to(powers, rows.shape[:-2] + (8, width))
    return jnp.concatenate([rows.astype(HALF), powers.astype(HALF)], axis=-2)


def without_exponents(pieces, count):
    return pieces[..., :count, :].astype(F32), pieces[..., count, :count].astype(F32)


def normalize(embed):
    norm = jnp.sqrt(jnp.sum(embed * embed, axis=1, keepdims=True) + 1e-06)
    return embed / norm, norm


def projected(grad, unit):
    return grad - unit * jnp.sum(unit * grad, axis=1, keepdims=True)


def shards(image_features, text_features, image_head, text_head, positive, log_scale, bias):
    rows = image_features.shape[0]
    planes = lax.axis_size(COLUMN)
    lanes = lax.axis_size("zl")
    quarter = rows // 4
    half = quarter // 2
    x, y, c = (lax.axis_index(name) for name in BLK)
    zh = lax.axis_index("zh")
    plane = zh * lanes + lax.axis_index("zl")
    image_part, text_part = plane // 4, plane % 4
    scale = jnp.exp(log_scale[0])
    offset = bias[0]

    def head_part(features, head):
        own = features.reshape(4, 2, half, -1)
        own = lax.dynamic_index_in_dim(own, zh, 1, keepdims=False).reshape(4 * half, -1)
        return jnp.dot(own, head, preferred_element_type=F32).reshape(4, half, -1)

    image_cols = head_part(image_features, image_head)
    text_cols = head_part(text_features, text_head)
    width = image_cols.shape[-1]
    image_powers = exponent(jnp.max(jnp.abs(image_cols), axis=-1))
    text_powers = exponent(jnp.max(jnp.abs(text_cols), axis=-1))
    image_cols = (image_cols * jnp.exp2(-image_powers)[..., None]).astype(HALF)
    text_cols = (text_cols * jnp.exp2(-text_powers)[..., None]).astype(HALF)

    def for_planes(image, text):
        image = jnp.broadcast_to(image[:, None], (4,) + image.shape)
        text = jnp.broadcast_to(text[None], (4,) + text.shape)
        return jnp.concatenate([image, text], axis=2).reshape((planes, quarter) + image.shape[3:])

    pieces = with_exponents(
        for_planes(image_cols, text_cols), for_planes(image_powers, text_powers)
    )
    pieces = lax.all_to_all(pieces, COLUMN, 0, 0, tiled=True)
    pieces, powers = without_exponents(pieces, quarter)
    pieces = pieces * jnp.exp2(powers)[..., None]
    pieces = pieces.reshape(2, lanes, 2, half, width)
    whole = pieces.transpose(2, 0, 3, 1, 4).reshape(2, quarter, lanes * width)
    image_unit, image_norm = normalize(whole[0])
    text_unit, text_norm = normalize(whole[1])

    text_b = text_unit.astype(jnp.bfloat16)
    image_b = spread(image_unit.astype(jnp.bfloat16), "y").reshape(8 * quarter, -1)
    text_own = jnp.concatenate([text_b] + [shifted(text_b, "x", k) for k in range(1, 4)])
    text_far = swapped(text_own)

    keys = positive.reshape(4, 8, 2, 4, quarter)
    keys = lax.dynamic_slice(keys, (x, 0, c, image_part, 0), (1, 8, 1, 1, quarter))
    keys = keys.reshape(1, 8 * quarter)

    def weights(text_b, core):
        logits = scale * jnp.einsum("ce,re->cr", text_b, image_b, preferred_element_type=F32)
        logits = logits + offset
        row = lax.broadcasted_iota(jnp.int32, (4 * quarter, 1), 0)
        block = (((x - row // quarter) & 3) * 8 + y) * 2 + core
        index = block * rows + text_part * quarter + row % quarter
        sign = jnp.where(keys == index, 1.0, -1.0)
        return (-sign * jax.nn.sigmoid(-sign * logits) * scale).astype(jnp.bfloat16)

    def to_texts(weight):
        return jnp.dot(weight, image_b, preferred_element_type=F32)

    def to_images(weight, text_b):
        return jnp.einsum("cr,ce->re", weight, text_b, preferred_element_type=F32)

    weight_far = weights(text_far, 1 - c)
    far_grad = swapped(to_texts(weight_far))
    weight_own = weights(text_own, c)
    image_grad = to_images(weight_far, text_far) + to_images(weight_own, text_own)
    text_grad = to_texts(weight_own) + far_grad

    text_parts = text_grad.astype(HALF).reshape(4, quarter, -1)
    text_grad = text_parts[0].astype(F32)
    for k in range(1, 4):
        text_grad = text_grad + shifted(text_parts[k], "x", -k).astype(F32)
    image_grad = summed(image_grad.astype(HALF), "y")

    both = jnp.stack([projected(image_grad, image_unit), projected(text_grad, text_unit)])
    norms = jnp.stack([image_norm, text_norm])
    powers = exponent(norms)
    both = both * (jnp.exp2(powers) / norms)
    both = both.reshape(2, quarter, lanes, width).transpose(0, 2, 1, 3)
    both = with_exponents(both, powers.reshape(2, 1, quarter)).reshape(planes, quarter + 8, width)
    both = lax.all_to_all(both, COLUMN, 0, 0, tiled=True)
    both, powers = without_exponents(both.reshape(4, 4, quarter + 8, width), quarter)
    powers = jnp.where(zh == 0, powers[:, 0], powers[0])
    result = jnp.where(zh == 0, jnp.sum(both, axis=1), jnp.sum(both, axis=0))
    result = result / jnp.exp2(powers)[:, :, None]
    return result.reshape(1, rows, width)


def solution(mesh):
    fine = Mesh(mesh.devices.reshape(4, 8, 2, 8, 2), AXES)
    placed = (P(BLK, None), P(BLK, None), P(None, "zl"), P(None, "zl"), P(), P(), P())
    return jax.shard_map(
        shards, mesh=fine, in_specs=placed, out_specs=P("zh", BLK, "zl"), check_vma=False
    )
```

```python
import jax
import jax.numpy as jnp
from jax import lax
from jax.sharding import Mesh, PartitionSpec as P

BLK = ("x", "y", "c")
AXES = BLK + ("zl", "zh")
COLUMN = ("zh", "zl")
F32 = jnp.float32
HALF = jnp.float16


def spread(value, axis):
    count = lax.axis_size(axis)
    copies = jnp.broadcast_to(value[None], (count,) + value.shape)
    return lax.all_to_all(copies, axis, 0, 0, tiled=True)


def summed(parts, axis):
    count = lax.axis_size(axis)
    parts = parts.reshape((count, -1) + parts.shape[1:])
    return jnp.sum(lax.all_to_all(parts, axis, 0, 0, tiled=True).astype(F32), axis=0)


def swapped(value):
    return lax.ppermute(value, "c", [(0, 1), (1, 0)])


def shifted(value, axis, steps):
    count = lax.axis_size(axis)
    return lax.ppermute(value, axis, [(k, (k + steps) % count) for k in range(count)])


def exponent(value):
    return jnp.clip(jnp.floor(jnp.log2(jnp.maximum(value, 1e-30))), -100.0, 126.0)


def with_exponents(rows, powers):
    count, width = rows.shape[-2:]
    lead = [(0, 0)] * (powers.ndim - 1)
    powers = jnp.pad(powers[..., None, :], lead + [(0, 7), (0, width - count)])
    powers = jnp.broadcast_to(powers, rows.shape[:-2] + (8, width))
    return jnp.concatenate([rows.astype(HALF), powers.astype(HALF)], axis=-2)


def without_exponents(pieces, count):
    return pieces[..., :count, :].astype(F32), pieces[..., count, :count].astype(F32)


def normalize(embed):
    norm = jnp.sqrt(jnp.sum(embed * embed, axis=1, keepdims=True) + 1e-06)
    return embed / norm, norm


def projected(grad, unit):
    return grad - unit * jnp.sum(unit * grad, axis=1, keepdims=True)


def shards(image_features, text_features, image_head, text_head, positive, log_scale, bias):
    rows = image_features.shape[0]
    planes = lax.axis_size(COLUMN)
    lanes = lax.axis_size("zl")
    quarter = rows // 4
    half = quarter // 2
    x, y, c = (lax.axis_index(name) for name in BLK)
    zh = lax.axis_index("zh")
    plane = zh * lanes + lax.axis_index("zl")
    image_part, text_part = plane // 4, plane % 4
    scale = jnp.exp(log_scale[0])
    offset = bias[0]

    def head_part(features, head):
        own = features.reshape(4, 2, half, -1)
        own = lax.dynamic_index_in_dim(own, zh, 1, keepdims=False).reshape(4 * half, -1)
        return jnp.dot(own, head, preferred_element_type=F32).reshape(4, half, -1)

    image_cols = head_part(image_features, image_head)
    text_cols = head_part(text_features, text_head)
    width = image_cols.shape[-1]
    image_powers = exponent(jnp.max(jnp.abs(image_cols), axis=-1))
    text_powers = exponent(jnp.max(jnp.abs(text_cols), axis=-1))
    image_cols = (image_cols * jnp.exp2(-image_powers)[..., None]).astype(HALF)
    text_cols = (text_cols * jnp.exp2(-text_powers)[..., None]).astype(HALF)

    def for_planes(image, text):
        image = jnp.broadcast_to(image[:, None], (4,) + image.shape)
        text = jnp.broadcast_to(text[None], (4,) + text.shape)
        return jnp.concatenate([image, text], axis=2).reshape((planes, quarter) + image.shape[3:])

    pieces = with_exponents(
        for_planes(image_cols, text_cols), for_planes(image_powers, text_powers)
    )
    pieces = lax.all_to_all(pieces, COLUMN, 0, 0, tiled=True)
    pieces, powers = without_exponents(pieces, quarter)
    pieces = pieces * jnp.exp2(powers)[..., None]
    pieces = pieces.reshape(2, lanes, 2, half, width)
    whole = pieces.transpose(2, 0, 3, 1, 4).reshape(2, quarter, lanes * width)
    image_unit, image_norm = normalize(whole[0])
    text_unit, text_norm = normalize(whole[1])

    text_b = text_unit.astype(jnp.bfloat16)
    image_b = spread(image_unit.astype(jnp.bfloat16), "y").reshape(8 * quarter, -1)
    text_own = jnp.concatenate([text_b] + [shifted(text_b, "x", k) for k in range(1, 4)])
    text_far = swapped(text_own)

    keys = positive.reshape(-1, 2 * rows)
    keys = lax.dynamic_slice(keys, (x * 8, c * rows + image_part * quarter), (8, quarter))
    keys = keys.reshape(1, 8 * quarter)
    key_block, key_row = keys // rows, keys % rows
    place = ((x - key_block // 16) & 3) * quarter + key_row % quarter
    place = place + jnp.where(key_block % 2 == c, 0, 4 * quarter)
    inside = (key_block // 2 % 8 == y) & (key_row // quarter == text_part)
    place = jnp.where(inside, place, -1)

    def weights(text_b, first):
        logits = scale * jnp.einsum("ce,re->cr", text_b, image_b, preferred_element_type=F32)
        logits = logits + offset
        index = lax.broadcasted_iota(jnp.int32, logits.shape, 0) + first
        sign = jnp.where(place == index, 1.0, -1.0)
        return (-sign * jax.nn.sigmoid(-sign * logits) * scale).astype(jnp.bfloat16)

    def to_texts(weight):
        return jnp.dot(weight, image_b, preferred_element_type=F32)

    def to_images(weight, text_b):
        return jnp.einsum("cr,ce->re", weight, text_b, preferred_element_type=F32)

    weight_own = weights(text_own, 0)
    image_grad = to_images(weight_own, text_own)
    text_far, weight_own, image_grad = lax.optimization_barrier((text_far, weight_own, image_grad))
    weight_far = weights(text_far, 4 * quarter)
    image_grad = (image_grad + to_images(weight_far, text_far)).astype(HALF)
    weight_own, weight_far, image_grad = lax.optimization_barrier(
        (weight_own, weight_far, image_grad)
    )
    far_grad = swapped(to_texts(weight_far))
    text_grad = to_texts(weight_own) + far_grad

    text_parts = text_grad.astype(HALF).reshape(4, quarter, -1)
    text_grad = text_parts[0].astype(F32)
    for k in range(1, 4):
        text_grad = text_grad + shifted(text_parts[k], "x", -k).astype(F32)
    image_grad = summed(image_grad, "y")

    both = jnp.stack([projected(image_grad, image_unit), projected(text_grad, text_unit)])
    norms = jnp.stack([image_norm, text_norm])
    powers = exponent(norms)
    both = both * (jnp.exp2(powers) / norms)
    both = both.reshape(2, quarter, lanes, width).transpose(0, 2, 1, 3)
    both = with_exponents(both, powers.reshape(2, 1, quarter)).reshape(planes, quarter + 8, width)
    both = lax.all_to_all(both, COLUMN, 0, 0, tiled=True)
    both, powers = without_exponents(both.reshape(4, 4, quarter + 8, width), quarter)
    powers = jnp.where(zh == 0, powers[:, 0], powers[0])
    result = jnp.where(zh == 0, jnp.sum(both, axis=1), jnp.sum(both, axis=0))
    result = result / jnp.exp2(powers)[:, :, None]
    return result.reshape(1, rows, width)


def solution(mesh):
    fine = Mesh(mesh.devices.reshape(4, 8, 2, 8, 2), AXES)
    placed = (P(BLK, None), P(BLK, None), P(None, "zl"), P(None, "zl"), P(), P(), P())
    return jax.shard_map(
        shards, mesh=fine, in_specs=placed, out_specs=P("zh", BLK, "zl"), check_vma=False
    )
```

```python
import jax
import jax.numpy as jnp
from jax import lax
from jax.sharding import Mesh, PartitionSpec as P

BLK = ("x", "ya", "yb", "c")
TEXT_GROUP = ("x", "yb")
AXES = BLK + ("zl", "zh")
COLUMN = ("zh", "zl")
F32 = jnp.float32
HALF = jnp.float16


def spread(value, axis):
    count = lax.axis_size(axis)
    copies = jnp.broadcast_to(value[None], (count,) + value.shape)
    return lax.all_to_all(copies, axis, 0, 0, tiled=True)


def summed(parts, axis):
    count = lax.axis_size(axis)
    parts = parts.reshape((count, -1) + parts.shape[1:])
    return jnp.sum(lax.all_to_all(parts, axis, 0, 0, tiled=True).astype(F32), axis=0)


def swapped(value):
    return lax.ppermute(value, "c", [(0, 1), (1, 0)])


def shifted(value, axis, steps):
    count = lax.axis_size(axis)
    return lax.ppermute(value, axis, [(k, (k + steps) % count) for k in range(count)])


def exponent(value):
    return jnp.clip(jnp.floor(jnp.log2(jnp.maximum(value, 1e-30))), -100.0, 126.0)


def with_exponents(rows, powers):
    count, width = rows.shape[-2:]
    lead = [(0, 0)] * (powers.ndim - 1)
    powers = jnp.pad(powers[..., None, :], lead + [(0, 7), (0, width - count)])
    powers = jnp.broadcast_to(powers, rows.shape[:-2] + (8, width))
    return jnp.concatenate([rows.astype(HALF), powers.astype(HALF)], axis=-2)


def without_exponents(pieces, count):
    return pieces[..., :count, :].astype(F32), pieces[..., count, :count].astype(F32)


def normalize(embed):
    norm = jnp.sqrt(jnp.sum(embed * embed, axis=1, keepdims=True) + 1e-06)
    return embed / norm, norm


def projected(grad, unit):
    return grad - unit * jnp.sum(unit * grad, axis=1, keepdims=True)


def shards(image_features, text_features, image_head, text_head, positive, log_scale, bias):
    rows = image_features.shape[0]
    planes = lax.axis_size(COLUMN)
    lanes = lax.axis_size("zl")
    quarter = rows // 4
    half = quarter // 2
    x, ya, yb, c = (lax.axis_index(name) for name in BLK)
    zh = lax.axis_index("zh")
    plane = zh * lanes + lax.axis_index("zl")
    image_part, text_part = plane // 4, plane % 4
    scale = jnp.exp(log_scale[0])
    offset = bias[0]

    def head_part(features, head):
        own = features.reshape(4, 2, half, -1)
        own = lax.dynamic_index_in_dim(own, zh, 1, keepdims=False).reshape(4 * half, -1)
        return jnp.dot(own, head, preferred_element_type=F32).reshape(4, half, -1)

    image_cols = head_part(image_features, image_head)
    text_cols = head_part(text_features, text_head)
    width = image_cols.shape[-1]
    image_powers = exponent(jnp.max(jnp.abs(image_cols), axis=-1))
    text_powers = exponent(jnp.max(jnp.abs(text_cols), axis=-1))
    image_cols = (image_cols * jnp.exp2(-image_powers)[..., None]).astype(HALF)
    text_cols = (text_cols * jnp.exp2(-text_powers)[..., None]).astype(HALF)

    def for_planes(image, text):
        image = jnp.broadcast_to(image[:, None], (4,) + image.shape)
        text = jnp.broadcast_to(text[None], (4,) + text.shape)
        return jnp.concatenate([image, text], axis=2).reshape((planes, quarter) + image.shape[3:])

    pieces = with_exponents(
        for_planes(image_cols, text_cols), for_planes(image_powers, text_powers)
    )
    pieces = lax.all_to_all(pieces, COLUMN, 0, 0, tiled=True)
    pieces, powers = without_exponents(pieces, quarter)
    pieces = pieces * jnp.exp2(powers)[..., None]
    pieces = pieces.reshape(2, lanes, 2, half, width)
    whole = pieces.transpose(2, 0, 3, 1, 4).reshape(2, quarter, lanes * width)
    image_unit, image_norm = normalize(whole[0])
    text_unit, text_norm = normalize(whole[1])

    text_own = spread(text_unit.astype(jnp.bfloat16), TEXT_GROUP).reshape(8 * quarter, -1)
    image_b = image_unit.astype(jnp.bfloat16)
    image_b = jnp.concatenate([image_b] + [shifted(image_b, "ya", k) for k in range(1, 4)])
    text_far = swapped(text_own)

    keys = positive.reshape(4, 4, 2, 2 * rows)
    keys = lax.dynamic_slice(keys, (x, 0, yb, c * rows + image_part * quarter), (1, 4, 1, quarter))
    keys = keys.reshape(4, quarter)[::-1]
    keys = lax.dynamic_slice(jnp.concatenate([keys, keys]), (3 - ya, 0), (4, quarter))
    keys = keys.reshape(1, 4 * quarter)
    key_block, key_row = keys // rows, keys % rows
    place = (key_block // 16 * 2 + key_block // 2 % 2) * quarter + key_row % quarter
    place = place + jnp.where(key_block % 2 == c, 0, 8 * quarter)
    inside = (key_block // 4 % 4 == ya) & (key_row // quarter == text_part)
    place = jnp.where(inside, place, -1)

    def weights(text_b, first):
        logits = scale * jnp.einsum("ce,re->cr", text_b, image_b, preferred_element_type=F32)
        logits = logits + offset
        index = lax.broadcasted_iota(jnp.int32, logits.shape, 0) + first
        sign = jnp.where(place == index, 1.0, -1.0)
        return (-sign * jax.nn.sigmoid(-sign * logits) * scale).astype(jnp.bfloat16)

    def to_texts(weight):
        return jnp.dot(weight, image_b, preferred_element_type=F32)

    def to_images(weight, text_b):
        return jnp.einsum("cr,ce->re", weight, text_b, preferred_element_type=F32)

    weight_far = weights(text_far, 8 * quarter)
    far_grad = swapped(to_texts(weight_far).astype(HALF))
    weight_own = weights(text_own, 0)
    text_grad = (to_texts(weight_own) + far_grad.astype(F32)).astype(HALF)
    weight_own, weight_far, text_grad = lax.optimization_barrier(
        (weight_own, weight_far, text_grad)
    )
    image_grad = to_images(weight_own, text_own) + to_images(weight_far, text_far)
    image_parts = image_grad.astype(HALF).reshape(4, quarter, -1)
    image_grad = image_parts[0].astype(F32)
    for k in range(1, 4):
        image_grad = image_grad + shifted(image_parts[k], "ya", -k).astype(F32)
    text_grad = summed(text_grad, TEXT_GROUP)

    both = jnp.stack([projected(image_grad, image_unit), projected(text_grad, text_unit)])
    norms = jnp.stack([image_norm, text_norm])
    powers = exponent(norms)
    both = both * (jnp.exp2(powers) / norms)
    both = both.reshape(2, quarter, lanes, width).transpose(0, 2, 1, 3)
    both = with_exponents(both, powers.reshape(2, 1, quarter)).reshape(planes, quarter + 8, width)
    both = lax.all_to_all(both, COLUMN, 0, 0, tiled=True)
    both, powers = without_exponents(both.reshape(4, 4, quarter + 8, width), quarter)
    powers = jnp.where(zh == 0, powers[:, 0], powers[0])
    result = jnp.where(zh == 0, jnp.sum(both, axis=1), jnp.sum(both, axis=0))
    result = result / jnp.exp2(powers)[:, :, None]
    return result.reshape(1, rows, width)


def solution(mesh):
    fine = Mesh(mesh.devices.reshape(4, 4, 2, 2, 8, 2), AXES)
    placed = (P(BLK, None), P(BLK, None), P(None, "zl"), P(None, "zl"), P(), P(), P())
    return jax.shard_map(
        shards, mesh=fine, in_specs=placed, out_specs=P("zh", BLK, "zl"), check_vma=False
    )
```

```python
import jax
import jax.numpy as jnp
from jax import lax
from jax.sharding import Mesh, PartitionSpec as P

BLK = ("x", "ya", "yb", "c")
IMAGE_GROUP = ("x", "yb")
AXES = BLK + ("zl", "zh")
COLUMN = ("zh", "zl")
F32 = jnp.float32
HALF = jnp.float16


def copies(value, axis):
    count = lax.axis_size(axis)
    return jnp.broadcast_to(value[None], (count,) + value.shape)


def exchanged(parts, axis):
    return lax.all_to_all(parts, axis, 0, 0, tiled=True)


def totals(parts):
    return jnp.sum(parts.astype(F32), axis=0)


def swapped(value):
    return lax.ppermute(value, "c", [(0, 1), (1, 0)])


def exponent(value):
    return jnp.clip(jnp.floor(jnp.log2(jnp.maximum(value, 1e-30))), -100.0, 126.0)


def with_exponents(rows, powers):
    count, width = rows.shape[-2:]
    lead = [(0, 0)] * (powers.ndim - 1)
    powers = jnp.pad(powers[..., None, :], lead + [(0, 7), (0, width - count)])
    powers = jnp.broadcast_to(powers, rows.shape[:-2] + (8, width))
    return jnp.concatenate([rows.astype(HALF), powers.astype(HALF)], axis=-2)


def without_exponents(pieces, count):
    return pieces[..., :count, :].astype(F32), pieces[..., count, :count].astype(F32)


def normalize(embed):
    norm = jnp.sqrt(jnp.sum(embed * embed, axis=1, keepdims=True) + 1e-06)
    return embed / norm, norm


def projected(grad, unit):
    return grad - unit * jnp.sum(unit * grad, axis=1, keepdims=True)


def shards(image_features, text_features, image_head, text_head, positive, log_scale, bias):
    rows = image_features.shape[0]
    planes = lax.axis_size(COLUMN)
    lanes = lax.axis_size("zl")
    quarter = rows // 4
    half = quarter // 2
    x, ya, yb, c = (lax.axis_index(name) for name in BLK)
    zh = lax.axis_index("zh")
    plane = zh * lanes + lax.axis_index("zl")
    image_part, text_part = plane // 4, plane % 4
    scale = jnp.exp(log_scale[0])
    offset = bias[0]

    def head_part(features, head):
        own = features.reshape(4, 2, half, -1)
        own = lax.dynamic_index_in_dim(own, zh, 1, keepdims=False).reshape(4 * half, -1)
        return jnp.dot(own, head, preferred_element_type=F32).reshape(4, half, -1)

    image_cols = head_part(image_features, image_head)
    text_cols = head_part(text_features, text_head)
    width = image_cols.shape[-1]
    image_powers = exponent(jnp.max(jnp.abs(image_cols), axis=-1))
    text_powers = exponent(jnp.max(jnp.abs(text_cols), axis=-1))
    image_cols = (image_cols * jnp.exp2(-image_powers)[..., None]).astype(HALF)
    text_cols = (text_cols * jnp.exp2(-text_powers)[..., None]).astype(HALF)

    def for_planes(image, text):
        image = jnp.broadcast_to(image[:, None], (4,) + image.shape)
        text = jnp.broadcast_to(text[None], (4,) + text.shape)
        return jnp.concatenate([image, text], axis=2).reshape((planes, quarter) + image.shape[3:])

    pieces = with_exponents(
        for_planes(image_cols, text_cols), for_planes(image_powers, text_powers)
    )
    pieces = exchanged(pieces, COLUMN)
    pieces, powers = without_exponents(pieces, quarter)
    pieces = pieces * jnp.exp2(powers)[..., None]
    pieces = pieces.reshape(2, lanes, 2, half, width)
    whole = pieces.transpose(2, 0, 3, 1, 4).reshape(2, quarter, lanes * width)
    image_unit, image_norm = normalize(whole[0])
    text_unit, text_norm = normalize(whole[1])

    text_own = copies(text_unit.astype(jnp.bfloat16), "ya")
    image_b = copies(image_unit.astype(jnp.bfloat16), IMAGE_GROUP)
    text_own, image_b = lax.optimization_barrier((text_own, image_b))
    text_own = exchanged(text_own, "ya")
    text_own, image_b, positive = lax.optimization_barrier((text_own, image_b, positive))
    text_own = text_own.reshape(4 * quarter, -1)
    text_far = swapped(text_own)
    image_b = exchanged(image_b, IMAGE_GROUP)
    image_b, text_far = lax.optimization_barrier((image_b, text_far))
    image_b = image_b.reshape(8 * quarter, -1)

    keys = positive.reshape(4, 4, 2, 2 * rows)
    keys = lax.dynamic_slice(keys, (0, ya, 0, c * rows + image_part * quarter), (4, 1, 2, quarter))
    keys = keys.reshape(1, 8 * quarter)
    key_block, key_row = keys // rows, keys % rows
    place = key_block // 4 % 4 * quarter + key_row % quarter
    place = place + jnp.where(key_block % 2 == c, 0, 4 * quarter)
    inside = (key_block // 16 == x) & (key_block // 2 % 2 == yb) & (key_row // quarter == text_part)
    place = jnp.where(inside, place, -1)

    def weights(text_b, first):
        logits = scale * jnp.einsum("ce,re->cr", text_b, image_b, preferred_element_type=F32)
        logits = logits + offset
        index = lax.broadcasted_iota(jnp.int32, logits.shape, 0) + first
        sign = jnp.where(place == index, 1.0, -1.0)
        return (-sign * jax.nn.sigmoid(-sign * logits) * scale).astype(jnp.bfloat16)

    def to_texts(weight):
        return jnp.dot(weight, image_b, preferred_element_type=F32)

    def to_images(weight, text_b):
        return jnp.einsum("cr,ce->re", weight, text_b, preferred_element_type=F32)

    weight_far = weights(text_far, 4 * quarter)
    far_grad = swapped(to_texts(weight_far))
    weight_own = weights(text_own, 0)
    image_grad = (to_images(weight_far, text_far) + to_images(weight_own, text_own)).astype(HALF)
    text_grad = (to_texts(weight_own) + far_grad).astype(HALF)

    image_grad = image_grad.reshape(8, quarter, -1)
    text_grad = text_grad.reshape(4, quarter, -1)
    powers = exponent(jnp.stack([image_norm, text_norm]))
    factors = jnp.exp2(powers) / jnp.stack([image_norm, text_norm])
    image_grad, text_grad, factors, powers, is_image = lax.optimization_barrier(
        (image_grad, text_grad, factors, powers, zh == 0)
    )
    text_grad = exchanged(text_grad, "ya")
    image_grad, text_grad = lax.optimization_barrier((image_grad, text_grad))
    image_grad = exchanged(image_grad, IMAGE_GROUP)
    image_grad, text_grad, factors, powers, is_image = lax.optimization_barrier(
        (image_grad, text_grad, factors, powers, is_image)
    )
    image_grad, text_grad = totals(image_grad), totals(text_grad)

    both = jnp.stack([projected(image_grad, image_unit), projected(text_grad, text_unit)])
    both = both * factors
    both = both.reshape(2, quarter, lanes, width).transpose(0, 2, 1, 3)
    both = with_exponents(both, powers.reshape(2, 1, quarter)).reshape(planes, quarter + 8, width)
    both, is_image = lax.optimization_barrier((both, is_image))
    both = exchanged(both, COLUMN)
    both, powers = without_exponents(both.reshape(4, 4, quarter + 8, width), quarter)
    powers = jnp.where(is_image, powers[:, 0], powers[0])
    result = jnp.where(is_image, jnp.sum(both, axis=1), jnp.sum(both, axis=0))
    result = result / jnp.exp2(powers)[:, :, None]
    return result.reshape(1, rows, width)


def solution(mesh):
    fine = Mesh(mesh.devices.reshape(4, 4, 2, 2, 8, 2), AXES)
    placed = (P(BLK, None), P(BLK, None), P(None, "zl"), P(None, "zl"), P(), P(), P())
    return jax.shard_map(
        shards, mesh=fine, in_specs=placed, out_specs=P("zh", BLK, "zl"), check_vma=False
    )
```

```python
import jax
import jax.numpy as jnp
from jax import lax
from jax.sharding import Mesh, PartitionSpec as P

BLK = ("x", "y", "c")
AXES = BLK + ("zl", "zh")
COLUMN = ("zh", "zl")
F32 = jnp.float32
HALF = jnp.float16


def spread(value, axis):
    count = lax.axis_size(axis)
    copies = jnp.broadcast_to(value[None], (count,) + value.shape)
    return lax.all_to_all(copies, axis, 0, 0, tiled=True)


def summed(parts, axis):
    count = lax.axis_size(axis)
    parts = parts.reshape((count, -1) + parts.shape[1:])
    return jnp.sum(lax.all_to_all(parts, axis, 0, 0, tiled=True).astype(F32), axis=0)


def swapped(value):
    return lax.ppermute(value, "c", [(0, 1), (1, 0)])


def shifted(value, axis, steps):
    count = lax.axis_size(axis)
    return lax.ppermute(value, axis, [(k, (k + steps) % count) for k in range(count)])


def exponent(value):
    return jnp.clip(jnp.floor(jnp.log2(jnp.maximum(value, 1e-30))), -100.0, 126.0)


def with_exponents(rows, powers):
    count, width = rows.shape[-2:]
    lead = [(0, 0)] * (powers.ndim - 1)
    powers = jnp.pad(powers[..., None, :], lead + [(0, 7), (0, width - count)])
    powers = jnp.broadcast_to(powers, rows.shape[:-2] + (8, width))
    return jnp.concatenate([rows.astype(HALF), powers.astype(HALF)], axis=-2)


def without_exponents(pieces, count):
    return pieces[..., :count, :].astype(F32), pieces[..., count, :count].astype(F32)


def normalize(embed):
    norm = jnp.sqrt(jnp.sum(embed * embed, axis=1, keepdims=True) + 1e-06)
    return embed / norm, norm


def projected(grad, unit):
    return grad - unit * jnp.sum(unit * grad, axis=1, keepdims=True)


def shards(image_features, text_features, image_head, text_head, positive, log_scale, bias):
    rows = image_features.shape[0]
    planes = lax.axis_size(COLUMN)
    lanes = lax.axis_size("zl")
    images, texts = rows // 8, rows // 2
    x, y, c = (lax.axis_index(name) for name in BLK)
    zh = lax.axis_index("zh")
    image_part, text_part = lax.axis_index("zl"), zh
    scale = jnp.exp(log_scale[0])
    offset = bias[0]

    text_rows = lax.dynamic_slice_in_dim(text_features, zh * texts, texts)
    image_cols = jnp.dot(image_features, image_head, preferred_element_type=F32)
    text_cols = jnp.dot(text_rows, text_head, preferred_element_type=F32)
    width = image_cols.shape[-1]

    def scaled(cols):
        powers = exponent(jnp.max(jnp.abs(cols), axis=-1))
        cols = (cols * jnp.exp2(-powers)[:, None]).reshape(-1, texts, width)
        return cols, powers.reshape(-1, texts)

    image_cols, image_powers = scaled(image_cols)
    text_cols, text_powers = scaled(text_cols)
    pieces = jnp.concatenate(
        [
            with_exponents(image_cols.reshape(8, images, width), image_powers.reshape(8, images)),
            jnp.broadcast_to(with_exponents(text_cols, text_powers), (8, texts + 8, width)),
        ],
        axis=1,
    )
    pieces = lax.all_to_all(pieces, "zl", 0, 0, tiled=True)

    def whole(part, count):
        part, powers = without_exponents(part, count)
        part = part * jnp.exp2(powers)[..., None]
        return part.transpose(1, 0, 2).reshape(count, lanes * width)

    image_unit, image_norm = normalize(whole(pieces[:, : images + 8], images))
    text_unit, text_norm = normalize(whole(pieces[:, images + 8 :], texts))

    text_b = text_unit.astype(jnp.bfloat16)
    image_own = spread(image_unit.astype(jnp.bfloat16), "y").reshape(8 * images, -1)
    text_b = jnp.concatenate([text_b] + [shifted(text_b, "x", k) for k in range(1, 4)])
    image_own, text_b = lax.optimization_barrier((image_own, text_b))
    image_far = swapped(image_own)

    def places(core):
        keys = positive.reshape(-1, 2 * rows)
        keys = lax.dynamic_slice(keys, (x * 8, core * rows + image_part * images), (8, images))
        keys = keys.reshape(1, 8 * images)
        block, row = keys // rows, keys % rows
        place = ((x - block // 16) & 3) * texts + row % texts
        inside = (block // 2 % 8 == y) & (block % 2 == c) & (row // texts == text_part)
        return jnp.where(inside, place, -1)

    def weights(image_b, place):
        logits = scale * jnp.einsum("ce,re->cr", text_b, image_b, preferred_element_type=F32)
        logits = logits + offset
        index = lax.broadcasted_iota(jnp.int32, logits.shape, 0)
        sign = jnp.where(place == index, 1.0, -1.0)
        return (-sign * jax.nn.sigmoid(-sign * logits) * scale).astype(jnp.bfloat16)

    def to_texts(weight, image_b):
        return jnp.dot(weight, image_b, preferred_element_type=F32)

    def to_images(weight):
        return jnp.einsum("cr,ce->re", weight, text_b, preferred_element_type=F32)

    weight_own = weights(image_own, places(c))
    own_grad = to_images(weight_own)
    image_far, weight_own, own_grad = lax.optimization_barrier((image_far, weight_own, own_grad))
    weight_far = weights(image_far, places(1 - c))
    image_grad = (own_grad + swapped(to_images(weight_far))).astype(HALF)
    text_grad = to_texts(weight_far, image_far) + to_texts(weight_own, image_own)

    text_parts = text_grad.astype(HALF).reshape(4, texts, -1)
    text_grad = text_parts[0].astype(F32)
    for k in range(1, 4):
        text_grad = text_grad + shifted(text_parts[k], "x", -k).astype(F32)
    image_grad = summed(image_grad, "y")

    def outgoing(grad, unit, norm):
        powers = exponent(norm) - 3.0
        piece = projected(grad, unit) * (jnp.exp2(powers) / norm)
        piece = piece.reshape(-1, lanes, width).transpose(1, 0, 2)
        powers = powers.reshape(1, -1)
        short = texts - powers.shape[1]
        piece = jnp.pad(piece, ((0, 0), (0, short), (0, 0)))
        return with_exponents(piece, jnp.pad(powers, ((0, 0), (0, short))))

    both = jnp.concatenate(
        [outgoing(image_grad, image_unit, image_norm), outgoing(text_grad, text_unit, text_norm)]
    )
    both = lax.all_to_all(both, COLUMN, 0, 0, tiled=True)
    both, powers = without_exponents(both.reshape(2, 8, texts + 8, width), texts)
    image_sum = jnp.sum(both[:, :, :images], axis=0) / jnp.exp2(powers[0, :, :images])[..., None]
    text_sum = jnp.sum(both, axis=1) / jnp.exp2(powers[:, 0])[..., None]
    image_sum, text_sum = image_sum.reshape(1, rows, width), text_sum.reshape(1, rows, width)
    return jnp.where(zh == 0, image_sum, text_sum)


def solution(mesh):
    fine = Mesh(mesh.devices.reshape(4, 8, 2, 8, 2), AXES)
    placed = (P(BLK, None), P(BLK, None), P(None, "zl"), P(None, "zl"), P(), P(), P())
    return jax.shard_map(
        shards, mesh=fine, in_specs=placed, out_specs=P("zh", BLK, "zl"), check_vma=False
    )
```

```python
import jax
import jax.numpy as jnp
from jax import lax
from jax.sharding import Mesh, PartitionSpec as P

BLK = ("x", "y", "c")
AXES = BLK + ("zl", "zh")
F32 = jnp.float32
HALF = jnp.float16


def spread(value, axis):
    count = lax.axis_size(axis)
    copies = jnp.broadcast_to(value[None], (count,) + value.shape)
    return lax.all_to_all(copies, axis, 0, 0, tiled=True)


def summed(parts, axis):
    count = lax.axis_size(axis)
    parts = parts.reshape((count, -1) + parts.shape[1:])
    return jnp.sum(lax.all_to_all(parts, axis, 0, 0, tiled=True).astype(F32), axis=0)


def swapped(value):
    return lax.ppermute(value, "c", [(0, 1), (1, 0)])


def shifted(value, axis, steps):
    count = lax.axis_size(axis)
    return lax.ppermute(value, axis, [(k, (k + steps) % count) for k in range(count)])


def exponent(value):
    return jnp.clip(jnp.floor(jnp.log2(jnp.maximum(value, 1e-30))), -100.0, 126.0)


def with_exponents(rows, powers):
    count, width = rows.shape[-2:]
    lead = [(0, 0)] * (powers.ndim - 1)
    powers = jnp.pad(powers[..., None, :], lead + [(0, 7), (0, width - count)])
    powers = jnp.broadcast_to(powers, rows.shape[:-2] + (8, width))
    return jnp.concatenate([rows.astype(HALF), powers.astype(HALF)], axis=-2)


def without_exponents(pieces, count):
    return pieces[..., :count, :].astype(F32), pieces[..., count, :count].astype(F32)


def normalize(embed):
    norm = jnp.sqrt(jnp.sum(embed * embed, axis=1, keepdims=True) + 1e-06)
    return embed / norm, norm


def projected(grad, unit):
    return grad - unit * jnp.sum(unit * grad, axis=1, keepdims=True)


def shards(image_features, text_features, image_head, text_head, positive, log_scale, bias):
    rows = image_features.shape[0]
    lanes = lax.axis_size("zl")
    owns, others = rows // 4, rows // 2
    x, y, c = (lax.axis_index(name) for name in BLK)
    is_image = lax.axis_index("zh") == 0
    plane = lax.axis_index("zl")
    own_part, other_part = plane // 2, plane % 2
    scale = jnp.exp(log_scale[0])
    offset = bias[0]

    image_cols = jnp.dot(image_features, image_head, preferred_element_type=F32)
    text_cols = jnp.dot(text_features, text_head, preferred_element_type=F32)
    width = image_cols.shape[-1]

    def scaled(cols):
        powers = exponent(jnp.max(jnp.abs(cols), axis=-1))
        return (cols * jnp.exp2(-powers)[:, None]).astype(HALF), powers.astype(HALF)

    image_cols, image_powers = scaled(image_cols)
    text_cols, text_powers = scaled(text_cols)

    def parted(image, text, powers_image, powers_text, count):
        cols = jnp.where(is_image, image, text).reshape(-1, count, width)
        powers = jnp.where(is_image, powers_image, powers_text).reshape(-1, count)
        return with_exponents(cols, powers)

    own = parted(image_cols, text_cols, image_powers, text_powers, owns)
    other = parted(text_cols, image_cols, text_powers, image_powers, others)
    own = jnp.broadcast_to(own[:, None], (4, 2) + own.shape[1:])
    other = jnp.broadcast_to(other[None], (4, 2) + other.shape[1:])
    pieces = jnp.concatenate([own, other], axis=2).reshape(lanes, -1, width)
    pieces = lax.all_to_all(pieces, "zl", 0, 0, tiled=True)

    def whole(part, count):
        part, powers = without_exponents(part, count)
        part = part * jnp.exp2(powers)[..., None]
        return part.transpose(1, 0, 2).reshape(count, lanes * width)

    own_unit, own_norm = normalize(whole(pieces[:, : owns + 8], owns))
    other_unit, _ = normalize(whole(pieces[:, owns + 8 :], others))

    own_b = spread(own_unit.astype(jnp.bfloat16), "y").reshape(8 * owns, -1)
    other_b = other_unit.astype(jnp.bfloat16)
    near_b = jnp.concatenate([other_b] + [shifted(other_b, "x", k) for k in range(1, 4)])
    far_b = swapped(near_b)

    table = positive.reshape(4, 8, 2 * rows)

    def keys(start, size, lane, count, image):
        found = lax.dynamic_slice(table, start + (lane,), size + (count,)).reshape(-1, count)
        block = start[0] + jnp.arange(size[0], dtype=jnp.int32)[:, None]
        block = block * 8 + start[1] + jnp.arange(size[1], dtype=jnp.int32)[None]
        index = block.reshape(-1, 1) * 2 * rows + lane + jnp.arange(count, dtype=jnp.int32)
        return jnp.where(image, found, index)

    own_keys = keys((x, 0), (1, 8), c * rows + own_part * owns, owns, is_image).reshape(1, -1)

    def other_keys(core):
        found = keys((0, y), (4, 1), core * rows + other_part * others, others, ~is_image)[::-1]
        found = jnp.concatenate([found, found])
        return lax.dynamic_slice_in_dim(found, 3 - x, 4).reshape(-1, 1)

    def gradient(b, key):
        logits = scale * jnp.einsum("ce,re->cr", b, own_b, preferred_element_type=F32) + offset
        sign = jnp.where(own_keys == key, 1.0, -1.0)
        weight = (-sign * jax.nn.sigmoid(-sign * logits) * scale).astype(jnp.bfloat16)
        return jnp.einsum("cr,ce->re", weight, b, preferred_element_type=F32)

    near_keys, far_keys = other_keys(c), other_keys(1 - c)
    grad = gradient(near_b, near_keys)
    grad, far_b, far_keys = lax.optimization_barrier((grad, far_b, far_keys))
    grad = summed((grad + gradient(far_b, far_keys)).astype(HALF), "y")

    powers = exponent(own_norm) - 3.0
    grad = projected(grad, own_unit) * (jnp.exp2(powers) / own_norm)
    grad = grad.reshape(owns, lanes, width).transpose(1, 0, 2)
    pieces = with_exponents(grad, powers.reshape(1, owns))
    pieces = lax.all_to_all(pieces, "zl", 0, 0, tiled=True)
    grad, powers = without_exponents(pieces.reshape(4, 2, owns + 8, width), owns)
    grad = jnp.sum(grad, axis=1) / jnp.exp2(powers[:, 0])[..., None]
    return grad.reshape(1, rows, width)


def solution(mesh):
    fine = Mesh(mesh.devices.reshape(4, 8, 2, 8, 2), AXES)
    placed = (P(BLK, None), P(BLK, None), P(None, "zl"), P(None, "zl"), P(), P(), P())
    return jax.shard_map(
        shards, mesh=fine, in_specs=placed, out_specs=P("zh", BLK, "zl"), check_vma=False
    )
```

```python
import jax
import jax.numpy as jnp
from jax import lax
from jax.sharding import Mesh, PartitionSpec as P

BLK = ("x", "y", "c")
AXES = BLK + ("zl", "zh")
F32 = jnp.float32
HALF = jnp.float16


def spread(value, axis):
    count = lax.axis_size(axis)
    copies = jnp.broadcast_to(value[None], (count,) + value.shape)
    return lax.all_to_all(copies, axis, 0, 0, tiled=True)


def summed(parts, axis):
    count = lax.axis_size(axis)
    parts = parts.reshape((count, -1) + parts.shape[1:])
    return jnp.sum(lax.all_to_all(parts, axis, 0, 0, tiled=True).astype(F32), axis=0)


def swapped(value):
    return lax.ppermute(value, "c", [(0, 1), (1, 0)])


def shifted(value, axis, steps):
    count = lax.axis_size(axis)
    return lax.ppermute(value, axis, [(k, (k + steps) % count) for k in range(count)])


def exponent(value):
    return jnp.clip(jnp.floor(jnp.log2(jnp.maximum(value, 1e-30))), -100.0, 126.0)


def with_exponents(rows, powers):
    count, width = rows.shape[-2:]
    lead = [(0, 0)] * (powers.ndim - 1)
    powers = jnp.pad(powers[..., None, :], lead + [(0, 7), (0, width - count)])
    powers = jnp.broadcast_to(powers, rows.shape[:-2] + (8, width))
    return jnp.concatenate([rows.astype(HALF), powers.astype(HALF)], axis=-2)


def without_exponents(pieces, count):
    return pieces[..., :count, :].astype(F32), pieces[..., count, :count].astype(F32)


def normalize(embed):
    norm = jnp.sqrt(jnp.sum(embed * embed, axis=1, keepdims=True) + 1e-06)
    return embed / norm, norm


def projected(grad, unit):
    return grad - unit * jnp.sum(unit * grad, axis=1, keepdims=True)


def shards(image_features, text_features, image_head, text_head, positive, log_scale, bias):
    rows = image_features.shape[0]
    lanes = lax.axis_size("zl")
    owns, others = rows // 2, rows // 4
    x, y, c = (lax.axis_index(name) for name in BLK)
    is_image = lax.axis_index("zh") == 0
    plane = lax.axis_index("zl")
    own_part, other_part = plane // 4, plane % 4
    scale = jnp.exp(log_scale[0])
    offset = bias[0]

    image_cols = jnp.dot(image_features, image_head, preferred_element_type=F32)
    text_cols = jnp.dot(text_features, text_head, preferred_element_type=F32)
    width = image_cols.shape[-1]

    def scaled(cols):
        powers = exponent(jnp.max(jnp.abs(cols), axis=-1))
        return (cols * jnp.exp2(-powers)[:, None]).astype(HALF), powers.astype(HALF)

    image_cols, image_powers = scaled(image_cols)
    text_cols, text_powers = scaled(text_cols)

    def parted(image, text, powers_image, powers_text, count):
        cols = jnp.where(is_image, image, text).reshape(-1, count, width)
        powers = jnp.where(is_image, powers_image, powers_text).reshape(-1, count)
        return with_exponents(cols, powers)

    own = parted(image_cols, text_cols, image_powers, text_powers, owns)
    other = parted(text_cols, image_cols, text_powers, image_powers, others)
    own = jnp.broadcast_to(own[:, None], (2, 4) + own.shape[1:])
    other = jnp.broadcast_to(other[None], (2, 4) + other.shape[1:])
    pieces = jnp.concatenate([own, other], axis=2).reshape(lanes, -1, width)
    pieces = lax.all_to_all(pieces, "zl", 0, 0, tiled=True)

    def whole(part, count):
        part, powers = without_exponents(part, count)
        part = part * jnp.exp2(powers)[..., None]
        return part.transpose(1, 0, 2).reshape(count, lanes * width)

    own_unit, own_norm = normalize(whole(pieces[:, : owns + 8], owns))
    other_unit, _ = normalize(whole(pieces[:, owns + 8 :], others))

    near_b = spread(other_unit.astype(jnp.bfloat16), "y").reshape(8 * others, -1)
    own_b = own_unit.astype(jnp.bfloat16)
    own_b = [shifted(own_b, "x", k) for k in (3, 2, 1)] + [own_b]
    own_b = jnp.concatenate(own_b + own_b[:3])
    own_b = lax.dynamic_slice_in_dim(own_b, (3 - x) * owns, 4 * owns)
    near_b, own_b = lax.optimization_barrier((near_b, own_b))
    far_b = swapped(near_b)

    table = positive.reshape(4, 8, 2 * rows)

    def keys(start, size, lane, count, image):
        found = lax.dynamic_slice(table, start + (lane,), size + (count,)).reshape(-1, count)
        block = start[0] + jnp.arange(size[0], dtype=jnp.int32)[:, None]
        block = block * 8 + start[1] + jnp.arange(size[1], dtype=jnp.int32)[None]
        index = block.reshape(-1, 1) * 2 * rows + lane + jnp.arange(count, dtype=jnp.int32)
        return jnp.where(image, found, index)

    own_keys = keys((0, y), (4, 1), c * rows + own_part * owns, owns, is_image).reshape(1, -1)

    def other_keys(core):
        lane = core * rows + other_part * others
        return keys((x, 0), (1, 8), lane, others, ~is_image).reshape(-1, 1)

    def gradient(b, key):
        logits = scale * jnp.einsum("ce,re->cr", b, own_b, preferred_element_type=F32) + offset
        sign = jnp.where(own_keys == key, 1.0, -1.0)
        weight = (-sign * jax.nn.sigmoid(-sign * logits) * scale).astype(jnp.bfloat16)
        weight = lax.optimization_barrier(weight)
        return jnp.einsum("cr,ce->re", weight, b, preferred_element_type=F32)

    near_keys, far_keys = other_keys(c), other_keys(1 - c)
    grad = gradient(near_b, near_keys)
    grad, far_b, far_keys = lax.optimization_barrier((grad, far_b, far_keys))
    grad = summed((grad + gradient(far_b, far_keys)).astype(HALF), "x")

    powers = exponent(own_norm) - 3.0
    grad = projected(grad, own_unit) * (jnp.exp2(powers) / own_norm)
    grad = grad.reshape(owns, lanes, width).transpose(1, 0, 2)
    pieces = with_exponents(grad, powers.reshape(1, owns))
    pieces = lax.all_to_all(pieces, "zl", 0, 0, tiled=True)
    grad, powers = without_exponents(pieces.reshape(2, 4, owns + 8, width), owns)
    grad = jnp.sum(grad, axis=1) / jnp.exp2(powers[:, 0])[..., None]
    return grad.reshape(1, rows, width)


def solution(mesh):
    fine = Mesh(mesh.devices.reshape(4, 8, 2, 8, 2), AXES)
    placed = (P(BLK, None), P(BLK, None), P(None, "zl"), P(None, "zl"), P(), P(), P())
    return jax.shard_map(
        shards, mesh=fine, in_specs=placed, out_specs=P("zh", BLK, "zl"), check_vma=False
    )
```

```python
import jax
import jax.numpy as jnp
from jax import lax
from jax.sharding import Mesh, PartitionSpec as P

BLK = ("x", "y", "c")
AXES = BLK + ("zl", "zh")
F32 = jnp.float32
HALF = jnp.float16


def spread(value, axis):
    count = lax.axis_size(axis)
    copies = jnp.broadcast_to(value[None], (count,) + value.shape)
    return lax.all_to_all(copies, axis, 0, 0, tiled=True)


def summed(parts, axis):
    count = lax.axis_size(axis)
    parts = parts.reshape((count, -1) + parts.shape[1:])
    return jnp.sum(lax.all_to_all(parts, axis, 0, 0, tiled=True).astype(F32), axis=0)


def swapped(value):
    return lax.ppermute(value, "c", [(0, 1), (1, 0)])


def shifted(value, axis, steps):
    count = lax.axis_size(axis)
    return lax.ppermute(value, axis, [(k, (k + steps) % count) for k in range(count)])


def exponent(value):
    return jnp.clip(jnp.floor(jnp.log2(jnp.maximum(value, 1e-30))), -100.0, 126.0)


def with_exponents(rows, powers):
    count, width = rows.shape[-2:]
    lead = [(0, 0)] * (powers.ndim - 1)
    powers = jnp.pad(powers[..., None, :], lead + [(0, 7), (0, width - count)])
    powers = jnp.broadcast_to(powers, rows.shape[:-2] + (8, width))
    return jnp.concatenate([rows.astype(HALF), powers.astype(HALF)], axis=-2)


def without_exponents(pieces, count):
    return pieces[..., :count, :].astype(F32), pieces[..., count, :count].astype(F32)


def normalize(embed):
    norm = jnp.sqrt(jnp.sum(embed * embed, axis=1, keepdims=True) + 1e-06)
    return embed / norm, norm


def projected(grad, unit):
    return grad - unit * jnp.sum(unit * grad, axis=1, keepdims=True)


def shards(image_features, text_features, image_head, text_head, positive, log_scale, bias):
    rows = image_features.shape[0]
    lanes = lax.axis_size("zl")
    owns, others = rows // 2, rows // 4
    x, y, c = (lax.axis_index(name) for name in BLK)
    is_image = lax.axis_index("zh") == 0
    plane = lax.axis_index("zl")
    own_part, other_part = plane // 4, plane % 4
    scale = jnp.exp(log_scale[0])
    offset = bias[0]

    text_cols = jnp.dot(text_features, text_head, preferred_element_type=F32)
    text_cols, image_features = lax.optimization_barrier((text_cols, image_features))
    image_cols = jnp.dot(image_features, image_head, preferred_element_type=F32)
    width = image_cols.shape[-1]

    def scaled(cols):
        powers = exponent(jnp.max(jnp.abs(cols), axis=-1))
        return (cols * jnp.exp2(-powers)[:, None]).astype(HALF), powers.astype(HALF)

    image_cols, image_powers = scaled(image_cols)
    text_cols, text_powers = scaled(text_cols)

    own_cols = jnp.where(is_image, image_cols, text_cols).reshape(2, 1, owns, width)
    other_cols = jnp.where(is_image, text_cols, image_cols).reshape(1, 4, others, width)
    own_powers = jnp.where(is_image, image_powers, text_powers).reshape(2, 1, 1, owns)
    other_powers = jnp.where(is_image, text_powers, image_powers).reshape(1, 4, 1, others)
    own_powers = jnp.pad(own_powers, ((0, 0), (0, 0), (0, 7), (0, width - owns)))
    other_powers = jnp.pad(other_powers, ((0, 0), (0, 0), (1, 6), (0, width - others)))
    pieces = [
        jnp.broadcast_to(own_cols, (2, 4, owns, width)),
        jnp.broadcast_to(other_cols, (2, 4, others, width)),
        own_powers + other_powers,
    ]
    pieces = jnp.concatenate(pieces, axis=2).reshape(lanes, -1, width)
    pieces = lax.all_to_all(pieces, "zl", 0, 0, tiled=True)

    def whole(part, powers):
        part = part.astype(F32) * jnp.exp2(powers.astype(F32))[..., None]
        return part.transpose(1, 0, 2).reshape(-1, lanes * width)

    received = owns + others
    own_unit, own_norm = normalize(whole(pieces[:, :owns], pieces[:, received, :owns]))
    other_unit, _ = normalize(
        whole(pieces[:, owns:received], pieces[:, received + 1, :others])
    )

    near_b = spread(other_unit.astype(jnp.bfloat16), "y").reshape(8 * others, -1)
    own_b = own_unit.astype(jnp.bfloat16)
    own_b = [shifted(own_b, "x", k) for k in (3, 2, 1)] + [own_b]
    own_b = jnp.concatenate(own_b + own_b[:3])
    own_b = lax.dynamic_slice_in_dim(own_b, (3 - x) * owns, 4 * owns)
    table = positive.reshape(4, 8, 2 * rows)

    def keys(start, size, lane, count, image):
        found = lax.dynamic_slice(table, start + (lane,), size + (count,)).reshape(-1, count)
        block = start[0] + jnp.arange(size[0], dtype=jnp.int32)[:, None]
        block = block * 8 + start[1] + jnp.arange(size[1], dtype=jnp.int32)[None]
        index = block.reshape(-1, 1) * 2 * rows + lane + jnp.arange(count, dtype=jnp.int32)
        return jnp.where(image, found, index)

    own_keys = keys((0, y), (4, 1), c * rows + own_part * owns, owns, is_image).reshape(1, -1)

    def other_keys(core):
        lane = core * rows + other_part * others
        return keys((x, 0), (1, 8), lane, others, ~is_image).reshape(-1, 1)

    def gradient(b, key):
        logits = scale * jnp.einsum("ce,re->cr", b, own_b, preferred_element_type=F32) + offset
        sign = jnp.where(own_keys == key, 1.0, -1.0)
        weight = (-sign * jax.nn.sigmoid(-sign * logits) * scale).astype(jnp.bfloat16)
        weight = lax.optimization_barrier(weight)
        return jnp.einsum("cr,ce->re", weight, b, preferred_element_type=F32)

    near_b, own_b, own_keys, near_keys, far_keys = lax.optimization_barrier(
        (near_b, own_b, own_keys, other_keys(c), other_keys(1 - c))
    )
    far_b = swapped(near_b)
    grad = gradient(near_b, near_keys)
    grad, far_b, far_keys = lax.optimization_barrier((grad, far_b, far_keys))
    grad = summed((grad + gradient(far_b, far_keys)).astype(HALF), "x")

    powers = exponent(own_norm) - 3.0
    grad = projected(grad, own_unit) * (jnp.exp2(powers) / own_norm)
    grad = grad.reshape(owns, lanes, width).transpose(1, 0, 2)
    pieces = with_exponents(grad, powers.reshape(1, owns))
    pieces = lax.all_to_all(pieces, "zl", 0, 0, tiled=True)
    grad, powers = without_exponents(pieces.reshape(2, 4, owns + 8, width), owns)
    grad = jnp.sum(grad, axis=1) / jnp.exp2(powers[:, 0])[..., None]
    return grad.reshape(1, rows, width)


def solution(mesh):
    fine = Mesh(mesh.devices.reshape(4, 8, 2, 8, 2), AXES)
    placed = (P(BLK, None), P(BLK, None), P(None, "zl"), P(None, "zl"), P(), P(), P())
    return jax.shard_map(
        shards, mesh=fine, in_specs=placed, out_specs=P("zh", BLK, "zl"), check_vma=False
    )
```

```python
import jax
import jax.numpy as jnp
from jax import lax
from jax.sharding import Mesh, PartitionSpec as P

BLK = ("x", "y", "c")
AXES = BLK + ("zl", "zh")
F32 = jnp.float32
HALF = jnp.float16


def spread(value, axis):
    count = lax.axis_size(axis)
    copies = jnp.broadcast_to(value[None], (count,) + value.shape)
    return lax.all_to_all(copies, axis, 0, 0, tiled=True)


def summed(parts, axis):
    count = lax.axis_size(axis)
    parts = parts.reshape((count, -1) + parts.shape[1:])
    return jnp.sum(lax.all_to_all(parts, axis, 0, 0, tiled=True).astype(F32), axis=0)


def swapped(value):
    return lax.ppermute(value, "c", [(0, 1), (1, 0)])


def shifted(value, axis, steps):
    count = lax.axis_size(axis)
    return lax.ppermute(value, axis, [(k, (k + steps) % count) for k in range(count)])


def exponent(value):
    return jnp.clip(jnp.floor(jnp.log2(jnp.maximum(value, 1e-30))), -100.0, 126.0)


def with_exponents(rows, powers):
    count, width = rows.shape[-2:]
    lead = [(0, 0)] * (powers.ndim - 1)
    powers = jnp.pad(powers[..., None, :], lead + [(0, 7), (0, width - count)])
    powers = jnp.broadcast_to(powers, rows.shape[:-2] + (8, width))
    return jnp.concatenate([rows.astype(HALF), powers.astype(HALF)], axis=-2)


def without_exponents(pieces, count):
    return pieces[..., :count, :].astype(F32), pieces[..., count, :count].astype(F32)


def normalize(embed):
    norm = jnp.sqrt(jnp.sum(embed * embed, axis=1, keepdims=True) + 1e-06)
    return embed / norm, norm


def projected(grad, unit):
    return grad - unit * jnp.sum(unit * grad, axis=1, keepdims=True)


def shards(image_features, text_features, image_head, text_head, positive, log_scale, bias):
    rows = image_features.shape[0]
    lanes = lax.axis_size("zl")
    owns, others = rows // 2, rows // 4
    x, y, c = (lax.axis_index(name) for name in BLK)
    is_image = lax.axis_index("zh") == 0
    plane = lax.axis_index("zl")
    own_part, other_part = plane // 4, plane % 4

    text_cols = jnp.dot(text_features, text_head, preferred_element_type=F32)
    text_cols, image_features = lax.optimization_barrier((text_cols, image_features))
    image_cols = jnp.dot(image_features, image_head, preferred_element_type=F32)
    width = image_cols.shape[-1]

    def scaled(cols):
        powers = exponent(jnp.max(jnp.abs(cols), axis=-1))
        return (cols * jnp.exp2(-powers)[:, None]).astype(HALF), powers.astype(HALF)

    image_cols, image_powers = scaled(image_cols)
    text_cols, text_powers = scaled(text_cols)

    own_cols = jnp.where(is_image, image_cols, text_cols).reshape(2, 1, owns, width)
    other_cols = jnp.where(is_image, text_cols, image_cols).reshape(1, 4, others, width)
    own_powers = jnp.where(is_image, image_powers, text_powers).reshape(2, 1, 1, owns)
    other_powers = jnp.where(is_image, text_powers, image_powers).reshape(1, 4, 1, others)
    own_powers = jnp.pad(own_powers, ((0, 0), (0, 0), (0, 7), (0, width - owns)))
    other_powers = jnp.pad(other_powers, ((0, 0), (0, 0), (1, 6), (0, width - others)))
    pieces = [
        jnp.broadcast_to(own_cols, (2, 4, owns, width)),
        jnp.broadcast_to(other_cols, (2, 4, others, width)),
        own_powers + other_powers,
    ]
    pieces = jnp.concatenate(pieces, axis=2).reshape(lanes, -1, width)
    pieces = lax.all_to_all(pieces, "zl", 0, 0, tiled=True)

    def whole(part, powers):
        part = part.astype(F32) * jnp.exp2(powers.astype(F32))[..., None]
        return part.transpose(1, 0, 2).reshape(-1, lanes * width)

    received = owns + others
    own_unit, own_norm = normalize(whole(pieces[:, :owns], pieces[:, received, :owns]))
    other_unit, _ = normalize(
        whole(pieces[:, owns:received], pieces[:, received + 1, :others])
    )

    near_b = spread(other_unit.astype(jnp.bfloat16), "y").reshape(8 * others, -1)
    own_b = own_unit.astype(jnp.bfloat16)
    own_b = [shifted(own_b, "x", k) for k in (3, 2, 1)] + [own_b]
    own_b = jnp.concatenate(own_b + own_b[:3])
    own_b = lax.dynamic_slice_in_dim(own_b, (3 - x) * owns, 4 * owns)
    table = positive.reshape(4, 8, 2 * rows)

    def keys(start, size, lane, count, image):
        found = lax.dynamic_slice(table, start + (lane,), size + (count,)).reshape(-1, count)
        block = start[0] + jnp.arange(size[0], dtype=jnp.int32)[:, None]
        block = block * 8 + start[1] + jnp.arange(size[1], dtype=jnp.int32)[None]
        index = block.reshape(-1, 1) * 2 * rows + lane + jnp.arange(count, dtype=jnp.int32)
        return jnp.where(image, found, index)

    own_keys = keys((0, y), (4, 1), c * rows + own_part * owns, owns, is_image).reshape(1, -1)

    def other_keys(core):
        lane = core * rows + other_part * others
        return keys((x, 0), (1, 8), lane, others, ~is_image).reshape(-1, 1)

    near_b, own_b, own_keys, near_keys, far_keys, scale, offset = lax.optimization_barrier(
        (near_b, own_b, own_keys, other_keys(c), other_keys(1 - c), jnp.exp(log_scale), bias)
    )
    scale, offset = scale[0], offset[0]
    far_b = swapped(near_b)

    def gradient(b, key):
        logits = scale * jnp.einsum("ce,re->cr", b, own_b, preferred_element_type=F32) + offset
        sign = jnp.where(own_keys == key, 1.0, -1.0)
        weight = (-sign * jax.nn.sigmoid(-sign * logits) * scale).astype(jnp.bfloat16)
        weight = lax.optimization_barrier(weight)
        return jnp.einsum("cr,ce->re", weight, b, preferred_element_type=F32)

    grad = gradient(near_b, near_keys)
    grad, far_b, far_keys = lax.optimization_barrier((grad, far_b, far_keys))
    grad = summed((grad + gradient(far_b, far_keys)).astype(HALF), "x")

    powers = exponent(own_norm) - 3.0
    grad = projected(grad, own_unit) * (jnp.exp2(powers) / own_norm)
    grad = grad.reshape(owns, lanes, width).transpose(1, 0, 2)
    pieces = with_exponents(grad, powers.reshape(1, owns))
    pieces = lax.all_to_all(pieces, "zl", 0, 0, tiled=True)
    grad, powers = without_exponents(pieces.reshape(2, 4, owns + 8, width), owns)
    grad = jnp.sum(grad, axis=1) / jnp.exp2(powers[:, 0])[..., None]
    return grad.reshape(1, rows, width)


def solution(mesh):
    fine = Mesh(mesh.devices.reshape(4, 8, 2, 8, 2), AXES)
    placed = (P(BLK, None), P(BLK, None), P(None, "zl"), P(None, "zl"), P(), P(), P())
    return jax.shard_map(
        shards, mesh=fine, in_specs=placed, out_specs=P("zh", BLK, "zl"), check_vma=False
    )
```

```python
import jax
import jax.numpy as jnp
from jax import lax
from jax.sharding import Mesh, PartitionSpec as P

BLK = ("x", "y", "c")
AXES = BLK + ("zl", "zh")
F32 = jnp.float32
HALF = jnp.float16


def spread(value, axis):
    count = lax.axis_size(axis)
    copies = jnp.broadcast_to(value[None], (count,) + value.shape)
    return lax.all_to_all(copies, axis, 0, 0, tiled=True)


def summed(parts, axis):
    count = lax.axis_size(axis)
    parts = parts.reshape((count, -1) + parts.shape[1:])
    return jnp.sum(lax.all_to_all(parts, axis, 0, 0, tiled=True).astype(F32), axis=0)


def swapped(value):
    return lax.ppermute(value, "c", [(0, 1), (1, 0)])


def shifted(value, axis, steps):
    count = lax.axis_size(axis)
    return lax.ppermute(value, axis, [(k, (k + steps) % count) for k in range(count)])


def exponent(value):
    return jnp.clip(jnp.floor(jnp.log2(jnp.maximum(value, 1e-30))), -100.0, 126.0)


def without_exponents(pieces, count):
    return pieces[..., :count, :].astype(F32), pieces[..., count, :count].astype(F32)


def normalize(embed):
    norm = jnp.sqrt(jnp.sum(embed * embed, axis=1, keepdims=True) + 1e-06)
    return embed / norm, norm


def projected(grad, unit):
    return grad - unit * jnp.sum(unit * grad, axis=1, keepdims=True)


def shards(image_features, text_features, image_head, text_head, positive, log_scale, bias):
    rows = image_features.shape[0]
    lanes = lax.axis_size("zl")
    owns, others = rows // 2, rows // 4
    x, y, c = (lax.axis_index(name) for name in BLK)
    is_image = lax.axis_index("zh") == 0
    plane = lax.axis_index("zl")
    own_part, other_part = plane // 4, plane % 4

    text_cols = jnp.dot(text_features, text_head, preferred_element_type=F32)
    text_cols, image_features = lax.optimization_barrier((text_cols, image_features))
    image_cols = jnp.dot(image_features, image_head, preferred_element_type=F32)
    width = image_cols.shape[-1]

    def scaled(cols):
        powers = exponent(jnp.max(jnp.abs(cols), axis=-1))
        return (cols * jnp.exp2(-powers)[:, None]).astype(HALF), powers.astype(HALF)

    image_cols, image_powers = scaled(image_cols)
    text_cols, text_powers = scaled(text_cols)

    own_cols = jnp.where(is_image, image_cols, text_cols).reshape(2, 1, owns, width)
    other_cols = jnp.where(is_image, text_cols, image_cols).reshape(1, 4, others, width)
    own_powers = jnp.where(is_image, image_powers, text_powers).reshape(2, 1, 1, owns)
    other_powers = jnp.where(is_image, text_powers, image_powers).reshape(1, 4, 1, others)
    own_powers = jnp.pad(own_powers, ((0, 0), (0, 0), (0, 7), (0, width - owns)))
    other_powers = jnp.pad(other_powers, ((0, 0), (0, 0), (1, 6), (0, width - others)))
    pieces = [
        jnp.broadcast_to(own_cols, (2, 4, owns, width)),
        jnp.broadcast_to(other_cols, (2, 4, others, width)),
        own_powers + other_powers,
    ]
    pieces = jnp.concatenate(pieces, axis=2).reshape(lanes, -1, width)
    pieces = lax.all_to_all(pieces, "zl", 0, 0, tiled=True)

    def whole(part, powers):
        part = part.astype(F32) * jnp.exp2(powers.astype(F32))[..., None]
        return part.transpose(1, 0, 2).reshape(-1, lanes * width)

    received = owns + others
    own_unit, own_norm = normalize(whole(pieces[:, :owns], pieces[:, received, :owns]))
    other_unit, _ = normalize(
        whole(pieces[:, owns:received], pieces[:, received + 1, :others])
    )

    near_b = spread(other_unit.astype(jnp.bfloat16), "y").reshape(8 * others, -1)
    own_b = own_unit.astype(jnp.bfloat16)
    own_b = [shifted(own_b, "x", k) for k in (3, 2, 1)] + [own_b]
    own_b = jnp.concatenate(own_b + own_b[:3])
    own_b = lax.dynamic_slice_in_dim(own_b, (3 - x) * owns, 4 * owns)
    table = positive.reshape(4, 8, 2 * rows)

    def keys(start, size, lane, count, image):
        found = lax.dynamic_slice(table, start + (lane,), size + (count,)).reshape(-1, count)
        block = start[0] + jnp.arange(size[0], dtype=jnp.int32)[:, None]
        block = block * 8 + start[1] + jnp.arange(size[1], dtype=jnp.int32)[None]
        index = block.reshape(-1, 1) * 2 * rows + lane + jnp.arange(count, dtype=jnp.int32)
        return jnp.where(image, found, index)

    own_keys = keys((0, y), (4, 1), c * rows + own_part * owns, owns, is_image).reshape(1, -1)

    def other_keys(core):
        lane = core * rows + other_part * others
        return keys((x, 0), (1, 8), lane, others, ~is_image).reshape(-1, 1)

    near_b, own_b, own_keys, near_keys, far_keys, scale, offset = lax.optimization_barrier(
        (near_b, own_b, own_keys, other_keys(c), other_keys(1 - c), jnp.exp(log_scale), bias)
    )
    scale, offset = scale[0], offset[0]
    far_b = swapped(near_b)

    def gradient(b, key):
        logits = scale * jnp.einsum("ce,re->cr", b, own_b, preferred_element_type=F32) + offset
        sign = jnp.where(own_keys == key, 1.0, -1.0)
        weight = (-sign * jax.nn.sigmoid(-sign * logits) * scale).astype(jnp.bfloat16)
        weight = lax.optimization_barrier(weight)
        return jnp.einsum("cr,ce->re", weight, b, preferred_element_type=F32)

    grad = gradient(near_b, near_keys)
    grad, far_b, far_keys = lax.optimization_barrier((grad, far_b, far_keys))
    grad = (grad + gradient(far_b, far_keys)).astype(HALF)

    powers = exponent(own_norm) - 3.0
    factors = jnp.exp2(powers) / own_norm
    power_rows = jnp.pad(powers.reshape(1, owns), ((0, 7), (0, width - owns))).astype(HALF)
    power_rows = jnp.broadcast_to(power_rows, (lanes, 8, width))
    grad, factors, power_rows = lax.optimization_barrier((grad, factors, power_rows))
    grad = projected(summed(grad, "x"), own_unit) * factors
    grad = grad.reshape(owns, lanes, width).transpose(1, 0, 2).astype(HALF)
    pieces = jnp.concatenate([grad, power_rows], axis=1)
    pieces = lax.all_to_all(pieces, "zl", 0, 0, tiled=True)
    grad, powers = without_exponents(pieces.reshape(2, 4, owns + 8, width), owns)
    grad = jnp.sum(grad, axis=1) / jnp.exp2(powers[:, 0])[..., None]
    return grad.reshape(1, rows, width)


def solution(mesh):
    fine = Mesh(mesh.devices.reshape(4, 8, 2, 8, 2), AXES)
    placed = (P(BLK, None), P(BLK, None), P(None, "zl"), P(None, "zl"), P(), P(), P())
    return jax.shard_map(
        shards, mesh=fine, in_specs=placed, out_specs=P("zh", BLK, "zl"), check_vma=False
    )
```
